32 devices in a mesh: groups: 2 (over y), row: 4 (over z), col: 4 (over x, core).
Axes of the slice: x: 2, y: 2, z: 4, core: 2. Of those that a mesh axis runs over, the one named last changes fastest.
Arguments:
- descriptors: float32 [32, 8192], P(None, ('groups', 'row', 'col')), parts along dimension 1, may hold values from -6 to 6
- lengthscale: float32 [64], P('groups'), parts along dimension 0, may hold values from 1.8 to 3.6
- noise: float32 [32], P('groups'), parts along dimension 0, may hold values from 0.1 to 1
- direction: float32 [16, 8192], P(None, ('groups', 'row', 'col')), parts along dimension 1, may hold values from -22 to 22
- residual: float32 [16, 8192], P(None, ('groups', 'row', 'col')), parts along dimension 1, may hold values from -22 to 22
- solution: float32 [16, 8192], P(None, ('groups', 'row', 'col')), parts along dimension 1, may hold values from -6 to 6
Outputs:
- new_solution: float32 [16, 8192], P(None, ('groups', 'row', 'col')), parts along dimension 1
- new_residual: float32 [16, 8192], P(None, ('groups', 'row', 'col')), parts along dimension 1
The draws below stay inside these ranges and needn't reach their ends.
There are 2 independent parts, one for each index of `groups`. The reference program is written for one: setup_inputs(seed, part) draws one part's arguments, and reference() takes and returns one part's arrays. A program takes and returns all parts, laid end to end along the dimension named above; each array names one. Nothing has to cross between parts.
All inputs are finite; a program needn't handle non-finite values.
Results may differ from the reference program's by a relative error of at most 0.000076.
Values sent between devices are 32-bit elements; how exact they have to be, the bound alone decides.
A program may use at most 64 MiB of HBM per device.

```python
import math
import jax
import jax.numpy as jnp
from jax import lax

PTS_DEV = 256
D = 32
RHS = 16
POINTS = 4096


def rising(key):
    place = jnp.arange(POINTS, dtype=jnp.float32) / POINTS
    level = jax.random.uniform(key, (POINTS,), jnp.float32)
    return jnp.exp(math.log(3.0) * (place - 0.5) + math.log(10.0) * (level - 0.5))


def draw_direction(key, part):
    key = jax.random.fold_in(key, 11)
    keys = jax.random.split(key, 3)
    base = jax.random.truncated_normal(keys[1], -4.0, 4.0, (RHS, POINTS), jnp.float32)
    return base * rising(keys[2])[None, :]


def draw_residual(key, part):
    key = jax.random.fold_in(key, 13)
    keys = jax.random.split(key, 3)
    base = jax.random.truncated_normal(keys[1], -4.0, 4.0, (RHS, POINTS), jnp.float32)
    return base * rising(keys[2])[None, :]


def level_of(own_key, shape, shards, smallest, top_value):
    def one(dim, parts):
        heights = jax.random.uniform(jax.random.fold_in(jax.random.fold_in(own_key, 6), dim), (parts,), jnp.float32, smallest / len(shards), top_value / len(shards))
        return jnp.repeat(jnp.exp(heights), shape[dim] // parts).reshape((-1,) + (1,) * (len(shape) - dim - 1))

    gain = one(*shards[0])
    for cut in shards[1:]:
        gain = gain * one(*cut)
    return gain


def normal_values(stream_key, extent, spread, limit, shards=(), kind=jnp.bfloat16):
    factor_of = level_of(stream_key, extent, shards, -0.22, 0.18) if shards else 1.0
    drawn = jax.random.normal(stream_key, extent, jnp.float32) * spread * factor_of
    return jnp.minimum(jnp.maximum(drawn, -limit), limit).astype(kind)


def setup_inputs(seed: int = 0, part: int = 0) -> dict:
    splits = jax.random.split(jax.random.key(seed), 7)
    own_keys = jax.random.split(jax.random.fold_in(splits[6], part), 7)
    return {
        "descriptors": normal_values(own_keys[0], (D, POINTS), 1.0, 6.0, ((1, 16),), jnp.float32),
        "lengthscale": jnp.clip(jnp.exp(jax.random.uniform(own_keys[1], (D,), jnp.float32, math.log(1.8), math.log(3.6))), 1.8, 3.6),
        "noise": jnp.clip(jnp.exp(jax.random.uniform(own_keys[2], (RHS,), jnp.float32, math.log(0.1), math.log(1.0))), 0.1, 1.0),
        "direction": draw_direction(jax.random.fold_in(jax.random.fold_in(splits[6], part), 71), part),
        "residual": draw_residual(jax.random.fold_in(jax.random.fold_in(splits[6], part), 71), part),
        "solution": normal_values(own_keys[5], (RHS, POINTS), 1.0, 6.0, ((1, 16),), jnp.float32),
    }


highest = lax.Precision.HIGHEST


def kernel_image(scaled, direction):
    squares = jnp.sum(scaled * scaled, axis=0)

    def one_block(offset):
        rows = lax.dynamic_slice_in_dim(scaled, offset, PTS_DEV, 1)
        row_squares = lax.dynamic_slice_in_dim(squares, offset, PTS_DEV, 0)
        cross = lax.dot_general(rows, scaled, (((0,), (0,)), ((), ())), precision=highest)
        kernel = jnp.exp(-0.5 * (row_squares[:, None] + squares[None, :] - 2.0 * cross))
        return lax.dot_general(direction, kernel, (((1,), (1,)), ((), ())), precision=highest)

    offsets = (jnp.arange(POINTS // PTS_DEV) * PTS_DEV).astype(jnp.int32)
    pieces = lax.map(one_block, offsets)
    return jnp.transpose(pieces, (1, 0, 2)).reshape(RHS, POINTS)


def reference(descriptors, lengthscale, noise, direction, residual, solution):
    scaled = descriptors / lengthscale[:, None]
    image = kernel_image(scaled, direction) + noise[:, None] * direction
    resid_sq = jnp.sum(residual * residual, axis=1)
    curvature = jnp.sum(direction * image, axis=1)
    alpha = resid_sq / curvature
    return solution + alpha[:, None] * direction, residual - alpha[:, None] * image
```

```python
import functools
import math

import jax
import jax.numpy as jnp
from jax import lax
from jax.experimental import pallas as pl
from jax.experimental.pallas import tpu as pltpu
from jax.sharding import PartitionSpec as P

MESH = pl.DeviceIdType.MESH
LOG2E = math.log2(math.e)
f32 = jnp.float32
bf16 = jnp.bfloat16


def split3(v):
    h = v.astype(bf16)
    rest = v - h.astype(f32)
    m = rest.astype(bf16)
    low = (rest - m.astype(f32)).astype(bf16)
    return h, m, low


def to_column(row, height):
    n = row.shape[1]
    wide = jnp.broadcast_to(row, (height, n))
    r = lax.broadcasted_iota(jnp.int32, (height, n), 0)
    c = lax.broadcasted_iota(jnp.int32, (height, n), 1)
    return jnp.sum(jnp.where(r == c, wide, 0.0), axis=1, keepdims=True)


def to_row(column, offset):
    h = column.shape[0]
    r = lax.broadcasted_iota(jnp.int32, (h, 128), 0)
    c = lax.broadcasted_iota(jnp.int32, (h, 128), 1)
    wide = jnp.broadcast_to(column, (h, 128))
    return jnp.sum(jnp.where(r + offset == c, wide, 0.0), axis=0, keepdims=True)


def half_square(x, xs):
    return -0.5 * jnp.sum(x * xs, axis=0, keepdims=True)


def square_rows(q, first):
    h, m, low = split3(q)
    n = q.shape[1]
    r = lax.broadcasted_iota(jnp.int32, (16, n), 0)
    base = 0 if first else 3
    other = (r >= 3 - base) & (r < 6 - base)
    out = jnp.where(other, 1.0, 0.0)
    for k, part in enumerate((h, m, low)):
        out = jnp.where(r == base + k, jnp.broadcast_to(part.astype(f32), (16, n)), out)
    return out.astype(bf16)


def stack_i(x):
    xs = x * LOG2E
    h, m, low = split3(xs)
    q = half_square(x, xs)
    pad = jnp.zeros((48, x.shape[1]), bf16)
    return jnp.concatenate([h, h, m, h, m, low, square_rows(q, True), pad], axis=0)


def stack_j(x):
    h, m, low = split3(x)
    q = half_square(x, x * LOG2E)
    pad = jnp.zeros((48, x.shape[1]), bf16)
    return jnp.concatenate([h, m, h, low, m, h, square_rows(q, False), pad], axis=0)


def kernel(R, C, x_ref, l_ref, n_ref, p_ref, r_ref, s_ref, sol_ref, res_ref,
           jbuf, ibuf, ist, part, rsbuf, stat,
           jsend, jrecv, isend, irecv, psend, precv, ssend, srecv):
    D, n = x_ref.shape
    H = p_ref.shape[0]
    my_row = lax.axis_index("row")
    my_col = lax.axis_index("col")

    def peer(dr, dc):
        return {"row": lax.rem(my_row + dr, R), "col": lax.rem(my_col + dc, C)}

    others = [(dr, dc) for dr in range(R) for dc in range(C) if dr or dc]
    barrier = pltpu.get_barrier_semaphore()
    for dr, dc in others:
        pl.semaphore_signal(barrier, inc=1, device_id=peer(dr, dc), device_id_type=MESH)

    jbuf[0, :D] = x_ref[...] / to_column(l_ref[...], D)
    jbuf[0, D:] = p_ref[...]
    noise = to_column(n_ref[...], H)

    pl.semaphore_wait(barrier, len(others))

    copies = []

    def remote(src, dst, send, recv, device):
        copy = pltpu.make_async_remote_copy(
            src_ref=src, dst_ref=dst, send_sem=send, recv_sem=recv,
            device_id=device, device_id_type=MESH)
        copy.start()
        copies.append(copy)
        return copy

    jcopy, icopy, pcopy, scopy = {}, {}, {}, {}
    for d in range(1, C):
        icopy[C - d] = remote(jbuf.at[0], ibuf.at[C - d], isend.at[C - d], irecv.at[C - d], peer(0, d))
    for d in range(1, R):
        jcopy[R - d] = remote(jbuf.at[0], jbuf.at[R - d], jsend.at[R - d], jrecv.at[R - d], peer(d, 0))

    resid = r_ref[...]
    resid_row = to_row(jnp.sum(resid * resid, axis=1, keepdims=True), H)
    mine = p_ref[...]
    curve = noise * mine * mine

    for jo in range(R):
        if jo:
            jcopy[jo].wait_recv()
        left = stack_j(jbuf[jo, :D])
        weights = jnp.concatenate(split3(jbuf[jo, D:]), axis=0)
        for s in range(C):
            if jo == 0:
                if s:
                    icopy[s].wait_recv()
                    ist[s] = stack_i(ibuf[s, :D])
                else:
                    ist[s] = stack_i(jbuf[0, :D])
            expo = lax.dot_general(left, ist[s], (((0,), (0,)), ((), ())), preferred_element_type=f32)
            k = jnp.exp2(expo)
            k1 = k.astype(bf16)
            k2 = (k - k1.astype(f32)).astype(bf16)
            got = jnp.dot(weights, k1, preferred_element_type=f32) + jnp.dot(weights, k2, preferred_element_type=f32)
            got = got[:H] + (got[H:2 * H] + got[2 * H:])
            if jo:
                got = part[s] + got
            part[s] = got
            if jo == R - 1:
                direction = ibuf[s, D:] if s else mine
                curve = curve + direction * got
                if s:
                    pcopy[C - s] = remote(part.at[s], rsbuf.at[C - s], psend.at[C - s], precv.at[C - s], peer(0, s))

    stat[0] = to_row(jnp.sum(curve, axis=1, keepdims=True), 0) + resid_row
    for dr, dc in others:
        slot = ((R - dr) % R) * C + (C - dc) % C
        scopy[slot] = remote(stat.at[0], stat.at[slot], ssend.at[slot], srecv.at[slot], peer(dr, dc))

    image = part[0] + noise * mine
    for s in range(1, C):
        pcopy[s].wait_recv()
        image = image + rsbuf[s]
    total = stat[0]
    for slot in range(1, R * C):
        scopy[slot].wait_recv()
        total = total + stat[slot]
    curvature = to_column(total, H)
    lane = lax.broadcasted_iota(jnp.int32, (H, 128), 1)
    sub = lax.broadcasted_iota(jnp.int32, (H, 128), 0)
    resid_sq = jnp.sum(jnp.where(lane == sub + H, jnp.broadcast_to(total, (H, 128)), 0.0), axis=1, keepdims=True)
    alpha = resid_sq / curvature
    sol_ref[...] = s_ref[...] + alpha * mine
    res_ref[...] = resid - alpha * image
    for copy in copies:
        copy.wait_send()


def shards(R, C, descriptors, lengthscale, noise, direction, residual, solution):
    D, n = descriptors.shape
    H = direction.shape[0]
    vmem = pl.BlockSpec(memory_space=pltpu.VMEM)
    dma = pltpu.SemaphoreType.DMA
    return pl.pallas_call(
        functools.partial(kernel, R, C),
        out_shape=(jax.ShapeDtypeStruct((H, n), f32), jax.ShapeDtypeStruct((H, n), f32)),
        in_specs=[vmem] * 6,
        out_specs=(vmem, vmem),
        scratch_shapes=[
            pltpu.VMEM((R, D + H, n), f32),
            pltpu.VMEM((C, D + H, n), f32),
            pltpu.VMEM((C, 256, n), bf16),
            pltpu.VMEM((C, H, n), f32),
            pltpu.VMEM((C, H, n), f32),
            pltpu.VMEM((R * C, 1, 128), f32),
            dma((R,)), dma((R,)), dma((C,)), dma((C,)),
            dma((C,)), dma((C,)), dma((R * C,)), dma((R * C,)),
        ],
        compiler_params=pltpu.CompilerParams(
            collective_id=0, has_side_effects=True, vmem_limit_bytes=32 * 1024 * 1024),
    )(descriptors, lengthscale.reshape(1, D), noise.reshape(1, H), direction, residual, solution)


def solution(mesh):
    spread = P(None, ("groups", "row", "col"))
    return jax.shard_map(
        functools.partial(shards, mesh.shape["row"], mesh.shape["col"]),
        mesh=mesh,
        in_specs=(spread, P("groups"), P("groups"), spread, spread, spread),
        out_specs=(spread, spread),
        check_vma=False,
    )
```

```python
import functools
import math

import jax
import jax.numpy as jnp
from jax import lax
from jax.experimental import pallas as pl
from jax.experimental.pallas import tpu as pltpu
from jax.sharding import PartitionSpec as P

MESH = pl.DeviceIdType.MESH
LOG2E = math.log2(math.e)
f32 = jnp.float32
bf16 = jnp.bfloat16


def split3(v):
    h = v.astype(bf16)
    rest = v - h.astype(f32)
    m = rest.astype(bf16)
    low = (rest - m.astype(f32)).astype(bf16)
    return h, m, low


def to_column(row, height):
    n = row.shape[1]
    wide = jnp.broadcast_to(row, (height, n))
    r = lax.broadcasted_iota(jnp.int32, (height, n), 0)
    c = lax.broadcasted_iota(jnp.int32, (height, n), 1)
    return jnp.sum(jnp.where(r == c, wide, 0.0), axis=1, keepdims=True)


def to_row(column, offset):
    h = column.shape[0]
    r = lax.broadcasted_iota(jnp.int32, (h, 128), 0)
    c = lax.broadcasted_iota(jnp.int32, (h, 128), 1)
    wide = jnp.broadcast_to(column, (h, 128))
    return jnp.sum(jnp.where(r + offset == c, wide, 0.0), axis=0, keepdims=True)


def half_square(x, xs):
    return -0.5 * jnp.sum(x * xs, axis=0, keepdims=True)


def square_rows(q, first):
    h, m, low = split3(q)
    n = q.shape[1]
    r = lax.broadcasted_iota(jnp.int32, (16, n), 0)
    base = 0 if first else 3
    other = (r >= 3 - base) & (r < 6 - base)
    out = jnp.where(other, 1.0, 0.0)
    for k, part in enumerate((h, m, low)):
        out = jnp.where(r == base + k, jnp.broadcast_to(part.astype(f32), (16, n)), out)
    return out.astype(bf16)


def stack_i(x):
    xs = x * LOG2E
    h, m, low = split3(xs)
    q = half_square(x, xs)
    pad = jnp.zeros((48, x.shape[1]), bf16)
    return jnp.concatenate([h, h, m, h, m, low, square_rows(q, True), pad], axis=0)


def stack_j(x):
    h, m, low = split3(x)
    q = half_square(x, x * LOG2E)
    pad = jnp.zeros((48, x.shape[1]), bf16)
    return jnp.concatenate([h, m, h, low, m, h, square_rows(q, False), pad], axis=0)


def kernel(R, C, x_hbm, l_hbm, n_hbm, p_hbm, r_hbm, alpha_ref, image_ref,
           xbuf, lbuf, nbuf, rbuf, jbuf, ibuf, ist, wbuf, back, backin, curve, part, rsbuf, stat,
           insem, bsend, brecv, jsend, jrecv, isend, irecv, psend, precv, ssend, srecv):
    D, n = x_hbm.shape
    H = p_hbm.shape[0]
    my_row = lax.axis_index("row")
    my_col = lax.axis_index("col")

    def peer(dr, dc):
        return {"row": lax.rem(my_row + dr, R), "col": lax.rem(my_col + dc, C)}

    half = R // 2
    upper = my_row // half
    takes_far = lax.rem(my_row + upper * (half + 1), 2) == 0
    others = [(dr, dc) for dr in range(R) for dc in range(C) if dr or dc]
    met = [(dr, 0) for dr in range(1, R)] + [(0, dc) for dc in range(1, C)]
    pairs = ((x_hbm, xbuf), (l_hbm, lbuf), (p_hbm, jbuf.at[0, D:]), (n_hbm, nbuf), (r_hbm, rbuf))
    loads = [pltpu.make_async_copy(src, dst, insem.at[k]) for k, (src, dst) in enumerate(pairs)]
    for load in loads:
        load.start()
    barrier = pltpu.get_barrier_semaphore()
    for dr, dc in met:
        pl.semaphore_signal(barrier, inc=1, device_id=peer(dr, dc), device_id_type=MESH)

    for load in loads[:3]:
        load.wait()
    jbuf[0, :D] = xbuf[...] / to_column(lbuf[...], D)

    pl.semaphore_wait(barrier, len(met))

    copies = []

    def describe(src, dst, send, recv, device):
        return pltpu.make_async_remote_copy(
            src_ref=src, dst_ref=dst, send_sem=send, recv_sem=recv,
            device_id=device, device_id_type=MESH)

    def remote(*spec):
        copy = describe(*spec)
        copy.start()
        copies.append(copy)
        return copy

    icopy, pcopy, scopy = {}, {}, {}
    jcopy = {d: describe(jbuf.at[0], jbuf.at[d], jsend.at[d], jrecv.at[d], peer(R - d, 0)) for d in range(1, half + 1)}
    bcopy = {d: describe(back.at[d], backin.at[d], bsend.at[d], brecv.at[d], peer(d, 0)) for d in range(1, half + 1)}
    for d in range(1, C):
        icopy[C - d] = remote(jbuf.at[0], ibuf.at[C - d], isend.at[C - d], irecv.at[C - d], peer(0, d))
    for d in range(1, half):
        jcopy[d].start()

    @pl.when(jnp.logical_not(takes_far))
    def _():
        jcopy[half].start()

    for load in loads[3:]:
        load.wait()
    noise = to_column(nbuf[...], H)
    resid = rbuf[...]
    resid_row = to_row(jnp.sum(resid * resid, axis=1, keepdims=True), H)
    mine = jbuf[0, D:]

    def tile(left, weights, s):
        expo = lax.dot_general(left, ist[s], (((0,), (0,)), ((), ())), preferred_element_type=f32)
        k = jnp.exp2(expo)
        k1 = k.astype(bf16)
        k2 = (k - k1.astype(f32)).astype(bf16)
        got = jnp.dot(weights, k1, preferred_element_type=f32) + jnp.dot(weights, k2, preferred_element_type=f32)
        return k1, k2, got[:H] + (got[H:2 * H] + got[2 * H:])

    left = stack_j(jbuf[0, :D])
    weights = jnp.concatenate(split3(mine), axis=0)
    wbuf[0] = weights
    for s in range(C):
        if s:
            icopy[s].wait_recv()
            ist[s] = stack_i(ibuf[s, :D])
            wbuf[s] = jnp.concatenate(split3(ibuf[s, D:]), axis=0)
        else:
            ist[s] = stack_i(jbuf[0, :D])
        part[s] = tile(left, weights, s)[2]

    curve[...] = noise * mine * mine

    def pair(d):
        jcopy[d].wait_recv()
        left = stack_j(jbuf[d, :D])
        weights = jnp.concatenate(split3(jbuf[d, D:]), axis=0)
        total = jnp.zeros((3 * H, n), f32)
        across = (((1,), (1,)), ((), ()))
        for s in range(C):
            k1, k2, got = tile(left, weights, s)
            part[s] += got
            total = total + lax.dot_general(wbuf[s], k1, across, preferred_element_type=f32)
            total = total + lax.dot_general(wbuf[s], k2, across, preferred_element_type=f32)
        total = total[:H] + (total[H:2 * H] + total[2 * H:])
        back[d] = total
        bcopy[d].start()
        curve[...] += jbuf[d, D:] * total

    for d in range(1, half):
        pair(d)

    @pl.when(takes_far)
    def _():
        pair(half)

    summed = curve[...] + mine * part[0]
    for s in range(1, C):
        pcopy[C - s] = remote(part.at[s], rsbuf.at[C - s], psend.at[C - s], precv.at[C - s], peer(0, s))
        summed = summed + ibuf[s, D:] * part[s]

    stat[0] = to_row(jnp.sum(summed, axis=1, keepdims=True), 0) + resid_row
    for dr, dc in others:
        slot = ((R - dr) % R) * C + (C - dc) % C
        scopy[slot] = remote(stat.at[0], stat.at[slot], ssend.at[slot], srecv.at[slot], peer(dr, dc))

    image = part[0] + noise * mine
    for s in range(1, C):
        pcopy[s].wait_recv()
        image = image + rsbuf[s]
    for d in range(1, half):
        bcopy[d].wait_recv()
        image = image + backin[d]
    alpha_ref[...] = jnp.zeros((H, n), f32)

    @pl.when(jnp.logical_not(takes_far))
    def _():
        bcopy[half].wait_recv()
        alpha_ref[...] = backin[half]

    image = image + alpha_ref[...]
    total = stat[0]
    for slot in range(1, R * C):
        scopy[slot].wait_recv()
        total = total + stat[slot]
    curvature = to_column(total, H)
    lane = lax.broadcasted_iota(jnp.int32, (H, 128), 1)
    sub = lax.broadcasted_iota(jnp.int32, (H, 128), 0)
    resid_sq = jnp.sum(jnp.where(lane == sub + H, jnp.broadcast_to(total, (H, 128)), 0.0), axis=1, keepdims=True)
    alpha = resid_sq / curvature
    alpha_ref[...] = jnp.broadcast_to(alpha, (H, n))
    image_ref[...] = image
    for copy in copies:
        copy.wait_send()
    for d in range(1, half):
        jcopy[d].wait_send()
        bcopy[d].wait_send()

    @pl.when(takes_far)
    def _():
        bcopy[half].wait_send()

    @pl.when(jnp.logical_not(takes_far))
    def _():
        jcopy[half].wait_send()


def shards(R, C, descriptors, lengthscale, noise, direction, residual, solution):
    D, n = descriptors.shape
    H = direction.shape[0]
    vmem = pl.BlockSpec(memory_space=pltpu.VMEM)
    dma = pltpu.SemaphoreType.DMA
    alpha, image = pl.pallas_call(
        functools.partial(kernel, R, C),
        out_shape=(jax.ShapeDtypeStruct((H, n), f32), jax.ShapeDtypeStruct((H, n), f32)),
        in_specs=[pl.BlockSpec(memory_space=pl.ANY)] * 5,
        out_specs=(vmem, vmem),
        scratch_shapes=[
            pltpu.VMEM((D, n), f32), pltpu.VMEM((1, D), f32), pltpu.VMEM((1, H), f32),
            pltpu.VMEM((H, n), f32),
            pltpu.VMEM((R, D + H, n), f32),
            pltpu.VMEM((C, D + H, n), f32),
            pltpu.VMEM((C, 256, n), bf16), pltpu.VMEM((C, 3 * H, n), bf16),
            pltpu.VMEM((R, H, n), f32), pltpu.VMEM((R, H, n), f32), pltpu.VMEM((H, n), f32),
            pltpu.VMEM((C, H, n), f32),
            pltpu.VMEM((C, H, n), f32),
            pltpu.VMEM((R * C, 1, 128), f32),
            dma((5,)), dma((R,)), dma((R,)), dma((R,)), dma((R,)), dma((C,)), dma((C,)),
            dma((C,)), dma((C,)), dma((R * C,)), dma((R * C,)),
        ],
        compiler_params=pltpu.CompilerParams(
            collective_id=0, has_side_effects=True, vmem_limit_bytes=64 * 1024 * 1024),
    )(descriptors, lengthscale.reshape(1, D), noise.reshape(1, H), direction, residual)
    return solution + alpha * direction, residual - alpha * image


def solution(mesh):
    spread = P(None, ("groups", "row", "col"))
    return jax.shard_map(
        functools.partial(shards, mesh.shape["row"], mesh.shape["col"]),
        mesh=mesh,
        in_specs=(spread, P("groups"), P("groups"), spread, spread, spread),
        out_specs=(spread, spread),
        check_vma=False,
    )
```

```python
import functools
import math

import jax
import jax.numpy as jnp
from jax import lax
from jax.experimental import pallas as pl
from jax.experimental.pallas import tpu as pltpu
from jax.sharding import PartitionSpec as P

MESH = pl.DeviceIdType.MESH
LOG2E = math.log2(math.e)
f32 = jnp.float32
bf16 = jnp.bfloat16


def split3(v):
    h = v.astype(bf16)
    rest = v - h.astype(f32)
    m = rest.astype(bf16)
    low = (rest - m.astype(f32)).astype(bf16)
    return h, m, low


def to_column(row, height):
    n = row.shape[1]
    wide = jnp.broadcast_to(row, (height, n))
    r = lax.broadcasted_iota(jnp.int32, (height, n), 0)
    c = lax.broadcasted_iota(jnp.int32, (height, n), 1)
    return jnp.sum(jnp.where(r == c, wide, 0.0), axis=1, keepdims=True)


def to_row(column, offset):
    h = column.shape[0]
    r = lax.broadcasted_iota(jnp.int32, (h, 128), 0)
    c = lax.broadcasted_iota(jnp.int32, (h, 128), 1)
    wide = jnp.broadcast_to(column, (h, 128))
    return jnp.sum(jnp.where(r + offset == c, wide, 0.0), axis=0, keepdims=True)


def half_square(x, xs):
    return -0.5 * jnp.sum(x * xs, axis=0, keepdims=True)


def square_rows(q, first):
    h, m, low = split3(q)
    n = q.shape[1]
    r = lax.broadcasted_iota(jnp.int32, (16, n), 0)
    base = 0 if first else 3
    other = (r >= 3 - base) & (r < 6 - base)
    out = jnp.where(other, 1.0, 0.0)
    for k, part in enumerate((h, m, low)):
        out = jnp.where(r == base + k, jnp.broadcast_to(part.astype(f32), (16, n)), out)
    return out.astype(bf16)


def stack_i(x):
    xs = x * LOG2E
    h, m, low = split3(xs)
    q = half_square(x, xs)
    pad = jnp.zeros((48, x.shape[1]), bf16)
    return jnp.concatenate([h, h, m, h, m, low, square_rows(q, True), pad], axis=0)


def stack_j(x):
    h, m, low = split3(x)
    q = half_square(x, x * LOG2E)
    pad = jnp.zeros((48, x.shape[1]), bf16)
    return jnp.concatenate([h, m, h, low, m, h, square_rows(q, False), pad], axis=0)


def kernel(R, C, x_hbm, l_hbm, n_hbm, p_hbm, r_hbm, alpha_ref, image_ref,
           xbuf, lbuf, nbuf, rbuf, jbuf, ibuf, ist, wbuf, back, backin, curve, part, rsbuf, stat,
           insem, bsend, brecv, jsend, jrecv, isend, irecv, psend, precv, ssend, srecv):
    D, n = x_hbm.shape
    H = p_hbm.shape[0]
    my_row = lax.axis_index("row")
    my_col = lax.axis_index("col")

    def peer(dr, dc):
        return {"row": lax.rem(my_row + dr, R), "col": lax.rem(my_col + dc, C)}

    half = R // 2
    upper = my_row // half
    takes_far = lax.rem(my_row + upper * (half + 1), 2) == 1
    others = [(dr, dc) for dr in range(R) for dc in range(C) if dr or dc]
    met = [(dr, 0) for dr in range(1, R)] + [(0, dc) for dc in range(1, C)]
    pairs = ((x_hbm, xbuf), (l_hbm, lbuf), (p_hbm, jbuf.at[0, D:]), (n_hbm, nbuf), (r_hbm, rbuf))
    loads = [pltpu.make_async_copy(src, dst, insem.at[k]) for k, (src, dst) in enumerate(pairs)]
    for load in loads:
        load.start()
    barrier = pltpu.get_barrier_semaphore()
    for dr, dc in met:
        pl.semaphore_signal(barrier, inc=1, device_id=peer(dr, dc), device_id_type=MESH)

    for load in loads[:3]:
        load.wait()
    jbuf[0, :D] = xbuf[...] / to_column(lbuf[...], D)

    pl.semaphore_wait(barrier, len(met))

    copies = []

    def describe(src, dst, send, recv, device):
        return pltpu.make_async_remote_copy(
            src_ref=src, dst_ref=dst, send_sem=send, recv_sem=recv,
            device_id=device, device_id_type=MESH)

    def remote(*spec):
        copy = describe(*spec)
        copy.start()
        copies.append(copy)
        return copy

    icopy, pcopy, scopy = {}, {}, {}
    jcopy = {d: describe(jbuf.at[0], jbuf.at[d], jsend.at[d], jrecv.at[d], peer(R - d, 0)) for d in range(1, half + 1)}
    bcopy = {d: describe(back.at[d], backin.at[d], bsend.at[d], brecv.at[d], peer(d, 0)) for d in range(1, half + 1)}
    for d in range(1, half):
        jcopy[d].start()

    @pl.when(jnp.logical_not(takes_far))
    def _():
        jcopy[half].start()

    for d in range(1, C):
        icopy[C - d] = remote(jbuf.at[0], ibuf.at[C - d], isend.at[C - d], irecv.at[C - d], peer(0, d))

    for load in loads[3:]:
        load.wait()
    noise = to_column(nbuf[...], H)
    resid = rbuf[...]
    resid_row = to_row(jnp.sum(resid * resid, axis=1, keepdims=True), H)
    mine = jbuf[0, D:]

    def tile(left, weights, s):
        expo = jnp.dot(left, ist[s], preferred_element_type=f32)
        k = jnp.exp2(expo)
        k1 = k.astype(bf16)
        k2 = (k - k1.astype(f32)).astype(bf16)
        got = jnp.dot(weights, k1, preferred_element_type=f32) + jnp.dot(weights, k2, preferred_element_type=f32)
        return k1, k2, got[:H] + (got[H:2 * H] + got[2 * H:])

    left = stack_j(jbuf[0, :D]).T
    weights = jnp.concatenate(split3(mine), axis=0)
    wbuf[0] = weights
    for s in range(C):
        if s:
            icopy[s].wait_recv()
            ist[s] = stack_i(ibuf[s, :D])
            wbuf[s] = jnp.concatenate(split3(ibuf[s, D:]), axis=0)
        else:
            ist[s] = stack_i(jbuf[0, :D])
        part[s] = tile(left, weights, s)[2]

    curve[...] = noise * mine * mine

    def pair(d):
        jcopy[d].wait_recv()
        left = stack_j(jbuf[d, :D]).T
        weights = jnp.concatenate(split3(jbuf[d, D:]), axis=0)
        total = jnp.zeros((3 * H, n), f32)
        across = (((1,), (1,)), ((), ()))
        for s in range(C):
            k1, k2, got = tile(left, weights, s)
            part[s] += got
            total = total + lax.dot_general(wbuf[s], k1, across, preferred_element_type=f32)
            total = total + lax.dot_general(wbuf[s], k2, across, preferred_element_type=f32)
        total = total[:H] + (total[H:2 * H] + total[2 * H:])
        back[d] = total
        bcopy[d].start()
        curve[...] += jbuf[d, D:] * total

    for d in range(1, half):
        pair(d)

    @pl.when(takes_far)
    def _():
        pair(half)

    summed = curve[...] + mine * part[0]
    for s in range(1, C):
        pcopy[C - s] = remote(part.at[s], rsbuf.at[C - s], psend.at[C - s], precv.at[C - s], peer(0, s))
        summed = summed + ibuf[s, D:] * part[s]

    stat[0] = to_row(jnp.sum(summed, axis=1, keepdims=True), 0) + resid_row
    for dr, dc in others:
        slot = ((R - dr) % R) * C + (C - dc) % C
        scopy[slot] = remote(stat.at[0], stat.at[slot], ssend.at[slot], srecv.at[slot], peer(dr, dc))

    image = part[0] + noise * mine
    for s in range(1, C):
        pcopy[s].wait_recv()
        image = image + rsbuf[s]
    for d in range(1, half):
        bcopy[d].wait_recv()
        image = image + backin[d]
    alpha_ref[...] = jnp.zeros((H, n), f32)

    @pl.when(jnp.logical_not(takes_far))
    def _():
        bcopy[half].wait_recv()
        alpha_ref[...] = backin[half]

    image = image + alpha_ref[...]
    total = stat[0]
    for slot in range(1, R * C):
        scopy[slot].wait_recv()
        total = total + stat[slot]
    curvature = to_column(total, H)
    lane = lax.broadcasted_iota(jnp.int32, (H, 128), 1)
    sub = lax.broadcasted_iota(jnp.int32, (H, 128), 0)
    resid_sq = jnp.sum(jnp.where(lane == sub + H, jnp.broadcast_to(total, (H, 128)), 0.0), axis=1, keepdims=True)
    alpha = resid_sq / curvature
    alpha_ref[...] = jnp.broadcast_to(alpha, (H, n))
    image_ref[...] = image
    for copy in copies:
        copy.wait_send()
    for d in range(1, half):
        jcopy[d].wait_send()
        bcopy[d].wait_send()

    @pl.when(takes_far)
    def _():
        bcopy[half].wait_send()

    @pl.when(jnp.logical_not(takes_far))
    def _():
        jcopy[half].wait_send()


def shards(R, C, descriptors, lengthscale, noise, direction, residual, solution):
    D, n = descriptors.shape
    H = direction.shape[0]
    vmem = pl.BlockSpec(memory_space=pltpu.VMEM)
    dma = pltpu.SemaphoreType.DMA
    alpha, image = pl.pallas_call(
        functools.partial(kernel, R, C),
        out_shape=(jax.ShapeDtypeStruct((H, n), f32), jax.ShapeDtypeStruct((H, n), f32)),
        in_specs=[pl.BlockSpec(memory_space=pl.ANY)] * 5,
        out_specs=(vmem, vmem),
        scratch_shapes=[
            pltpu.VMEM((D, n), f32), pltpu.VMEM((1, D), f32), pltpu.VMEM((1, H), f32),
            pltpu.VMEM((H, n), f32),
            pltpu.VMEM((R, D + H, n), f32),
            pltpu.VMEM((C, D + H, n), f32),
            pltpu.VMEM((C, 256, n), bf16), pltpu.VMEM((C, 3 * H, n), bf16),
            pltpu.VMEM((R, H, n), f32), pltpu.VMEM((R, H, n), f32), pltpu.VMEM((H, n), f32),
            pltpu.VMEM((C, H, n), f32),
            pltpu.VMEM((C, H, n), f32),
            pltpu.VMEM((R * C, 1, 128), f32),
            dma((5,)), dma((R,)), dma((R,)), dma((R,)), dma((R,)), dma((C,)), dma((C,)),
            dma((C,)), dma((C,)), dma((R * C,)), dma((R * C,)),
        ],
        compiler_params=pltpu.CompilerParams(
            collective_id=0, has_side_effects=True, vmem_limit_bytes=64 * 1024 * 1024),
    )(descriptors, lengthscale.reshape(1, D), noise.reshape(1, H), direction, residual)
    return solution + alpha * direction, residual - alpha * image


def solution(mesh):
    spread = P(None, ("groups", "row", "col"))
    return jax.shard_map(
        functools.partial(shards, mesh.shape["row"], mesh.shape["col"]),
        mesh=mesh,
        in_specs=(spread, P("groups"), P("groups"), spread, spread, spread),
        out_specs=(spread, spread),
        check_vma=False,
    )
```

```python
import functools
import math

import jax
import jax.numpy as jnp
from jax import lax
from jax.experimental import pallas as pl
from jax.experimental.pallas import tpu as pltpu
from jax.sharding import PartitionSpec as P

MESH = pl.DeviceIdType.MESH
LOG2E = math.log2(math.e)
f32 = jnp.float32
bf16 = jnp.bfloat16


def split3(v):
    h = v.astype(bf16)
    rest = v - h.astype(f32)
    m = rest.astype(bf16)
    low = (rest - m.astype(f32)).astype(bf16)
    return h, m, low


def to_column(row, height):
    n = row.shape[1]
    wide = jnp.broadcast_to(row, (height, n))
    r = lax.broadcasted_iota(jnp.int32, (height, n), 0)
    c = lax.broadcasted_iota(jnp.int32, (height, n), 1)
    return jnp.sum(jnp.where(r == c, wide, 0.0), axis=1, keepdims=True)


def to_row(column, offset):
    h = column.shape[0]
    r = lax.broadcasted_iota(jnp.int32, (h, 128), 0)
    c = lax.broadcasted_iota(jnp.int32, (h, 128), 1)
    wide = jnp.broadcast_to(column, (h, 128))
    return jnp.sum(jnp.where(r + offset == c, wide, 0.0), axis=0, keepdims=True)


def half_square(x, xs):
    return -0.5 * jnp.sum(x * xs, axis=0, keepdims=True)


def square_rows(q, first):
    h, m, low = split3(q)
    n = q.shape[1]
    r = lax.broadcasted_iota(jnp.int32, (16, n), 0)
    base = 0 if first else 3
    other = (r >= 3 - base) & (r < 6 - base)
    out = jnp.where(other, 1.0, 0.0)
    for k, part in enumerate((h, m, low)):
        out = jnp.where(r == base + k, jnp.broadcast_to(part.astype(f32), (16, n)), out)
    return out.astype(bf16)


def stack_i(x):
    xs = x * LOG2E
    h, m, low = split3(xs)
    q = half_square(x, xs)
    pad = jnp.zeros((48, x.shape[1]), bf16)
    return jnp.concatenate([h, h, m, h, m, low, square_rows(q, True), pad], axis=0)


def stack_j(x):
    h, m, low = split3(x)
    q = half_square(x, x * LOG2E)
    pad = jnp.zeros((48, x.shape[1]), bf16)
    return jnp.concatenate([h, m, h, low, m, h, square_rows(q, False), pad], axis=0)


def kernel(R, C, x_hbm, l_hbm, n_hbm, p_hbm, r_hbm, alpha_ref, image_ref,
           xbuf, lbuf, nbuf, rbuf, jbuf, ibuf, ist, wbuf, back, backin, curve, part, rsbuf, stat,
           insem, bsend, brecv, jsend, jrecv, isend, irecv, psend, precv, ssend, srecv):
    D, n = x_hbm.shape
    H = p_hbm.shape[0]
    my_row = lax.axis_index("row")
    my_col = lax.axis_index("col")

    def peer(dr, dc):
        return {"row": lax.rem(my_row + dr, R), "col": lax.rem(my_col + dc, C)}

    half = R // 2
    upper = my_row // half
    takes_far = lax.rem(my_row + upper * (half + 1), 2) == 1
    others = [(dr, dc) for dr in range(R) for dc in range(C) if dr or dc]
    met = [(dr, 0) for dr in range(1, R)] + [(0, dc) for dc in range(1, C)]
    pairs = ((x_hbm, xbuf), (l_hbm, lbuf), (p_hbm, jbuf.at[0, D:]), (n_hbm, nbuf), (r_hbm, rbuf))
    loads = [pltpu.make_async_copy(src, dst, insem.at[k]) for k, (src, dst) in enumerate(pairs)]
    for load in loads:
        load.start()
    barrier = pltpu.get_barrier_semaphore()
    for dr, dc in met:
        pl.semaphore_signal(barrier, inc=1, device_id=peer(dr, dc), device_id_type=MESH)

    for load in loads[:3]:
        load.wait()
    jbuf[0, :D] = xbuf[...] / to_column(lbuf[...], D)

    pl.semaphore_wait(barrier, len(met))

    copies = []

    def describe(src, dst, send, recv, device):
        return pltpu.make_async_remote_copy(
            src_ref=src, dst_ref=dst, send_sem=send, recv_sem=recv,
            device_id=device, device_id_type=MESH)

    def remote(*spec):
        copy = describe(*spec)
        copy.start()
        copies.append(copy)
        return copy

    icopy, pcopy, scopy = {}, {}, {}
    jcopy = {d: describe(jbuf.at[0], jbuf.at[d], jsend.at[d], jrecv.at[d], peer(R - d, 0)) for d in range(1, half + 1)}
    bcopy = {d: describe(back.at[d], backin.at[d], bsend.at[d], brecv.at[d], peer(d, 0)) for d in range(1, half + 1)}
    for d in range(1, half):
        jcopy[d].start()

    @pl.when(jnp.logical_not(takes_far))
    def _():
        jcopy[half].start()

    for d in range(1, C):
        icopy[C - d] = remote(jbuf.at[0], ibuf.at[C - d], isend.at[C - d], irecv.at[C - d], peer(0, d))

    for load in loads[3:]:
        load.wait()
    noise = to_column(nbuf[...], H)
    resid = rbuf[...]
    resid_row = to_row(jnp.sum(resid * resid, axis=1, keepdims=True), H)
    mine = jbuf[0, D:]

    def tile(left, weights, s):
        expo = jnp.dot(left, ist[s], preferred_element_type=f32)
        k = jnp.exp2(expo)
        k1 = k.astype(bf16)
        k2 = (k - k1.astype(f32)).astype(bf16)
        got = jnp.dot(weights, k1, preferred_element_type=f32) + jnp.dot(weights, k2, preferred_element_type=f32)
        return k1, k2, got[:H] + (got[H:2 * H] + got[2 * H:])

    left = stack_j(jbuf[0, :D]).T
    weights = jnp.concatenate(split3(mine), axis=0)
    wbuf[0] = weights
    for s in range(C):
        if s:
            icopy[s].wait_recv()
            ist[s] = stack_i(ibuf[s, :D])
            wbuf[s] = jnp.concatenate(split3(ibuf[s, D:]), axis=0)
        else:
            ist[s] = stack_i(jbuf[0, :D])
        part[s] = tile(left, weights, s)[2]

    curve[...] = noise * mine * mine

    def pair(d):
        jcopy[d].wait_recv()
        left = stack_j(jbuf[d, :D]).T
        weights = jnp.concatenate(split3(jbuf[d, D:]), axis=0)
        total = jnp.zeros((3 * H, n), f32)
        minor = jnp.zeros((2 * H, n), f32)
        across = (((1,), (1,)), ((), ()))
        for s in range(C):
            k1, k2, got = tile(left, weights, s)
            part[s] += got
            total = total + lax.dot_general(wbuf[s], k1, across, preferred_element_type=f32)
            minor = minor + lax.dot_general(wbuf[s, :2 * H], k2, across, preferred_element_type=f32)
        total = total[:H] + (total[H:2 * H] + total[2 * H:]) + (minor[:H] + minor[H:])
        back[d] = total
        bcopy[d].start()
        curve[...] += jbuf[d, D:] * total

    for d in range(1, half):
        pair(d)

    @pl.when(takes_far)
    def _():
        pair(half)

    summed = curve[...] + mine * part[0]
    for s in range(1, C):
        pcopy[C - s] = remote(part.at[s], rsbuf.at[C - s], psend.at[C - s], precv.at[C - s], peer(0, s))
        summed = summed + ibuf[s, D:] * part[s]

    stat[0] = to_row(jnp.sum(summed, axis=1, keepdims=True), 0) + resid_row
    for dr, dc in others:
        slot = ((R - dr) % R) * C + (C - dc) % C
        scopy[slot] = remote(stat.at[0], stat.at[slot], ssend.at[slot], srecv.at[slot], peer(dr, dc))

    image = part[0] + noise * mine
    for s in range(1, C):
        pcopy[s].wait_recv()
        image = image + rsbuf[s]
    for d in range(1, half):
        bcopy[d].wait_recv()
        image = image + backin[d]
    alpha_ref[...] = jnp.zeros((H, n), f32)

    @pl.when(jnp.logical_not(takes_far))
    def _():
        bcopy[half].wait_recv()
        alpha_ref[...] = backin[half]

    image = image + alpha_ref[...]
    total = stat[0]
    for slot in range(1, R * C):
        scopy[slot].wait_recv()
        total = total + stat[slot]
    curvature = to_column(total, H)
    lane = lax.broadcasted_iota(jnp.int32, (H, 128), 1)
    sub = lax.broadcasted_iota(jnp.int32, (H, 128), 0)
    resid_sq = jnp.sum(jnp.where(lane == sub + H, jnp.broadcast_to(total, (H, 128)), 0.0), axis=1, keepdims=True)
    alpha = resid_sq / curvature
    alpha_ref[...] = jnp.broadcast_to(alpha, (H, n))
    image_ref[...] = image
    for copy in copies:
        copy.wait_send()
    for d in range(1, half):
        jcopy[d].wait_send()
        bcopy[d].wait_send()

    @pl.when(takes_far)
    def _():
        bcopy[half].wait_send()

    @pl.when(jnp.logical_not(takes_far))
    def _():
        jcopy[half].wait_send()


def shards(R, C, descriptors, lengthscale, noise, direction, residual, solution):
    D, n = descriptors.shape
    H = direction.shape[0]
    vmem = pl.BlockSpec(memory_space=pltpu.VMEM)
    dma = pltpu.SemaphoreType.DMA
    alpha, image = pl.pallas_call(
        functools.partial(kernel, R, C),
        out_shape=(jax.ShapeDtypeStruct((H, n), f32), jax.ShapeDtypeStruct((H, n), f32)),
        in_specs=[pl.BlockSpec(memory_space=pl.ANY)] * 5,
        out_specs=(vmem, vmem),
        scratch_shapes=[
            pltpu.VMEM((D, n), f32), pltpu.VMEM((1, D), f32), pltpu.VMEM((1, H), f32),
            pltpu.VMEM((H, n), f32),
            pltpu.VMEM((R, D + H, n), f32),
            pltpu.VMEM((C, D + H, n), f32),
            pltpu.VMEM((C, 256, n), bf16), pltpu.VMEM((C, 3 * H, n), bf16),
            pltpu.VMEM((R, H, n), f32), pltpu.VMEM((R, H, n), f32), pltpu.VMEM((H, n), f32),
            pltpu.VMEM((C, H, n), f32),
            pltpu.VMEM((C, H, n), f32),
            pltpu.VMEM((R * C, 1, 128), f32),
            dma((5,)), dma((R,)), dma((R,)), dma((R,)), dma((R,)), dma((C,)), dma((C,)),
            dma((C,)), dma((C,)), dma((R * C,)), dma((R * C,)),
        ],
        compiler_params=pltpu.CompilerParams(
            collective_id=0, has_side_effects=True, vmem_limit_bytes=64 * 1024 * 1024),
    )(descriptors, lengthscale.reshape(1, D), noise.reshape(1, H), direction, residual)
    return solution + alpha * direction, residual - alpha * image


def solution(mesh):
    spread = P(None, ("groups", "row", "col"))
    return jax.shard_map(
        functools.partial(shards, mesh.shape["row"], mesh.shape["col"]),
        mesh=mesh,
        in_specs=(spread, P("groups"), P("groups"), spread, spread, spread),
        out_specs=(spread, spread),
        check_vma=False,
    )
```

```python
import functools
import math

import jax
import jax.numpy as jnp
from jax import lax
from jax.experimental import pallas as pl
from jax.experimental.pallas import tpu as pltpu
from jax.sharding import PartitionSpec as P

MESH = pl.DeviceIdType.MESH
LOG2E = math.log2(math.e)
f32 = jnp.float32
bf16 = jnp.bfloat16


def split3(v):
    h = v.astype(bf16)
    rest = v - h.astype(f32)
    m = rest.astype(bf16)
    low = (rest - m.astype(f32)).astype(bf16)
    return h, m, low


def to_column(row, height):
    n = row.shape[1]
    wide = jnp.broadcast_to(row, (height, n))
    r = lax.broadcasted_iota(jnp.int32, (height, n), 0)
    c = lax.broadcasted_iota(jnp.int32, (height, n), 1)
    return jnp.sum(jnp.where(r == c, wide, 0.0), axis=1, keepdims=True)


def to_row(column, offset):
    h = column.shape[0]
    r = lax.broadcasted_iota(jnp.int32, (h, 128), 0)
    c = lax.broadcasted_iota(jnp.int32, (h, 128), 1)
    wide = jnp.broadcast_to(column, (h, 128))
    return jnp.sum(jnp.where(r + offset == c, wide, 0.0), axis=0, keepdims=True)


def half_square(x, xs):
    return -0.5 * jnp.sum(x * xs, axis=0, keepdims=True)


def square_rows(q, first):
    h, m, low = split3(q)
    n = q.shape[1]
    r = lax.broadcasted_iota(jnp.int32, (16, n), 0)
    base = 0 if first else 3
    other = (r >= 3 - base) & (r < 6 - base)
    out = jnp.where(other, 1.0, 0.0)
    for k, part in enumerate((h, m, low)):
        out = jnp.where(r == base + k, jnp.broadcast_to(part.astype(f32), (16, n)), out)
    return out.astype(bf16)


def stack_i(x):
    xs = x * LOG2E
    h, m, low = split3(xs)
    q = half_square(x, xs)
    pad = jnp.zeros((48, x.shape[1]), bf16)
    return jnp.concatenate([h, h, m, h, m, low, square_rows(q, True), pad], axis=0)


def stack_j(x):
    h, m, low = split3(x)
    q = half_square(x, x * LOG2E)
    pad = jnp.zeros((48, x.shape[1]), bf16)
    return jnp.concatenate([h, m, h, low, m, h, square_rows(q, False), pad], axis=0)


def kernel(R, C, x_hbm, l_hbm, n_hbm, p_hbm, r_hbm, alpha_ref, image_ref,
           xbuf, lbuf, nbuf, rbuf, jbuf, ibuf, ist, wbuf, back, backin, curve, part, rsbuf, stat,
           insem, bsend, brecv, jsend, jrecv, isend, irecv, psend, precv, ssend, srecv):
    D, n = x_hbm.shape
    H = p_hbm.shape[0]
    my_row = lax.axis_index("row")
    my_col = lax.axis_index("col")

    def peer(dr, dc):
        return {"row": lax.rem(my_row + dr, R), "col": lax.rem(my_col + dc, C)}

    half = R // 2
    upper = my_row // half
    takes_far = lax.rem(my_row + upper * (half + 1), 2) == 1
    others = [(dr, dc) for dr in range(R) for dc in range(C) if dr or dc]
    met = [(dr, 0) for dr in range(1, R)] + [(0, dc) for dc in range(1, C)]
    pairs = ((x_hbm, xbuf), (l_hbm, lbuf), (p_hbm, jbuf.at[0, D:]), (n_hbm, nbuf), (r_hbm, rbuf))
    loads = [pltpu.make_async_copy(src, dst, insem.at[k]) for k, (src, dst) in enumerate(pairs)]
    for load in loads[:3]:
        load.start()
    barrier = pltpu.get_barrier_semaphore()
    for dr, dc in met:
        pl.semaphore_signal(barrier, inc=1, device_id=peer(dr, dc), device_id_type=MESH)

    for load in loads[3:]:
        load.start()
    for load in loads[:3]:
        load.wait()
    jbuf[0, :D] = xbuf[...] / to_column(lbuf[...], D)

    pl.semaphore_wait(barrier, len(met))

    copies = []

    def describe(src, dst, send, recv, device):
        return pltpu.make_async_remote_copy(
            src_ref=src, dst_ref=dst, send_sem=send, recv_sem=recv,
            device_id=device, device_id_type=MESH)

    def remote(*spec):
        copy = describe(*spec)
        copy.start()
        copies.append(copy)
        return copy

    icopy, pcopy, scopy = {}, {}, {}
    jcopy = {d: describe(jbuf.at[0], jbuf.at[d], jsend.at[d], jrecv.at[d], peer(R - d, 0)) for d in range(1, half + 1)}
    bcopy = {d: describe(back.at[d], backin.at[d], bsend.at[d], brecv.at[d], peer(d, 0)) for d in range(1, half + 1)}
    for d in range(1, half):
        jcopy[d].start()

    @pl.when(jnp.logical_not(takes_far))
    def _():
        jcopy[half].start()

    for d in range(1, C):
        icopy[C - d] = remote(jbuf.at[0], ibuf.at[C - d], isend.at[C - d], irecv.at[C - d], peer(0, d))

    for load in loads[3:]:
        load.wait()
    noise = to_column(nbuf[...], H)
    resid = rbuf[...]
    resid_row = to_row(jnp.sum(resid * resid, axis=1, keepdims=True), H)
    mine = jbuf[0, D:]

    def tile(left, weights, s):
        expo = jnp.dot(left, ist[s], preferred_element_type=f32)
        k = jnp.exp2(expo)
        k1 = k.astype(bf16)
        k2 = (k - k1.astype(f32)).astype(bf16)
        got = jnp.dot(weights, k1, preferred_element_type=f32) + jnp.dot(weights, k2, preferred_element_type=f32)
        return k1, k2, got[:H] + (got[H:2 * H] + got[2 * H:])

    left = stack_j(jbuf[0, :D]).T
    weights = jnp.concatenate(split3(mine), axis=0)
    wbuf[0] = weights
    for s in range(C):
        if s:
            icopy[s].wait_recv()
            ist[s] = stack_i(ibuf[s, :D])
            wbuf[s] = jnp.concatenate(split3(ibuf[s, D:]), axis=0)
        else:
            ist[s] = stack_i(jbuf[0, :D])
        part[s] = tile(left, weights, s)[2]

    curve[...] = noise * mine * mine

    def pair(d):
        jcopy[d].wait_recv()
        left = stack_j(jbuf[d, :D]).T
        weights = jnp.concatenate(split3(jbuf[d, D:]), axis=0)
        total = jnp.zeros((3 * H, n), f32)
        minor = jnp.zeros((2 * H, n), f32)
        across = (((1,), (1,)), ((), ()))
        for s in range(C):
            k1, k2, got = tile(left, weights, s)
            part[s] += got
            total = total + lax.dot_general(wbuf[s], k1, across, preferred_element_type=f32)
            minor = minor + lax.dot_general(wbuf[s, :2 * H], k2, across, preferred_element_type=f32)
        total = total[:H] + (total[H:2 * H] + total[2 * H:]) + (minor[:H] + minor[H:])
        back[d] = total
        bcopy[d].start()
        curve[...] += jbuf[d, D:] * total

    for d in range(1, half):
        pair(d)

    @pl.when(takes_far)
    def _():
        pair(half)

    summed = curve[...] + mine * part[0]
    for s in range(1, C):
        summed = summed + ibuf[s, D:] * part[s]

    stat[0] = to_row(jnp.sum(summed, axis=1, keepdims=True), 0) + resid_row
    for dr, dc in reversed(others):
        slot = ((R - dr) % R) * C + (C - dc) % C
        scopy[slot] = remote(stat.at[0], stat.at[slot], ssend.at[slot], srecv.at[slot], peer(dr, dc))

    for s in range(1, C):
        pcopy[C - s] = remote(part.at[s], rsbuf.at[C - s], psend.at[C - s], precv.at[C - s], peer(0, s))

    image = part[0] + noise * mine
    for s in range(1, C):
        pcopy[s].wait_recv()
        image = image + rsbuf[s]
    for d in range(1, half):
        bcopy[d].wait_recv()
        image = image + backin[d]
    alpha_ref[...] = jnp.zeros((H, n), f32)

    @pl.when(jnp.logical_not(takes_far))
    def _():
        bcopy[half].wait_recv()
        alpha_ref[...] = backin[half]

    image = image + alpha_ref[...]
    total = stat[0]
    for slot in range(1, R * C):
        scopy[slot].wait_recv()
        total = total + stat[slot]
    curvature = to_column(total, H)
    lane = lax.broadcasted_iota(jnp.int32, (H, 128), 1)
    sub = lax.broadcasted_iota(jnp.int32, (H, 128), 0)
    resid_sq = jnp.sum(jnp.where(lane == sub + H, jnp.broadcast_to(total, (H, 128)), 0.0), axis=1, keepdims=True)
    alpha = resid_sq / curvature
    alpha_ref[...] = jnp.broadcast_to(alpha, (H, n))
    image_ref[...] = image
    for copy in copies:
        copy.wait_send()
    for d in range(1, half):
        jcopy[d].wait_send()
        bcopy[d].wait_send()

    @pl.when(takes_far)
    def _():
        bcopy[half].wait_send()

    @pl.when(jnp.logical_not(takes_far))
    def _():
        jcopy[half].wait_send()


def shards(R, C, descriptors, lengthscale, noise, direction, residual, solution):
    D, n = descriptors.shape
    H = direction.shape[0]
    vmem = pl.BlockSpec(memory_space=pltpu.VMEM)
    dma = pltpu.SemaphoreType.DMA
    alpha, image = pl.pallas_call(
        functools.partial(kernel, R, C),
        out_shape=(jax.ShapeDtypeStruct((H, n), f32), jax.ShapeDtypeStruct((H, n), f32)),
        in_specs=[pl.BlockSpec(memory_space=pl.ANY)] * 5,
        out_specs=(vmem, vmem),
        scratch_shapes=[
            pltpu.VMEM((D, n), f32), pltpu.VMEM((1, D), f32), pltpu.VMEM((1, H), f32),
            pltpu.VMEM((H, n), f32),
            pltpu.VMEM((R, D + H, n), f32),
            pltpu.VMEM((C, D + H, n), f32),
            pltpu.VMEM((C, 256, n), bf16), pltpu.VMEM((C, 3 * H, n), bf16),
            pltpu.VMEM((R, H, n), f32), pltpu.VMEM((R, H, n), f32), pltpu.VMEM((H, n), f32),
            pltpu.VMEM((C, H, n), f32),
            pltpu.VMEM((C, H, n), f32),
            pltpu.VMEM((R * C, 1, 128), f32),
            dma((5,)), dma((R,)), dma((R,)), dma((R,)), dma((R,)), dma((C,)), dma((C,)),
            dma((C,)), dma((C,)), dma((R * C,)), dma((R * C,)),
        ],
        compiler_params=pltpu.CompilerParams(
            collective_id=0, has_side_effects=True, vmem_limit_bytes=64 * 1024 * 1024),
    )(descriptors, lengthscale.reshape(1, D), noise.reshape(1, H), direction, residual)
    return solution + alpha * direction, residual - alpha * image


def solution(mesh):
    spread = P(None, ("groups", "row", "col"))
    return jax.shard_map(
        functools.partial(shards, mesh.shape["row"], mesh.shape["col"]),
        mesh=mesh,
        in_specs=(spread, P("groups"), P("groups"), spread, spread, spread),
        out_specs=(spread, spread),
        check_vma=False,
    )
```
